32 devices in a mesh: seq: 8 (over z, x), head: 4 (over y, core).
Axes of the slice: x: 2, y: 2, z: 4, core: 2. Of those that a mesh axis runs over, the one named last changes fastest.
Arguments:
- queries: bfloat16 [4096, 1024], P('seq', 'head'), may hold values from -6 to 6
- keys: bfloat16 [4096, 1024], P('seq', 'head'), may hold values from -5 to 5
- values: bfloat16 [4096, 1024], P('seq', 'head'), may hold values from -6 to 6
- ridge: float32 [8], P('head'), may hold values from 0.5 to 4
- gain: float32 [1024], P('head'), may hold values from 0.5 to 1.5
- grad_out: bfloat16 [4096, 1024], P('seq', 'head'), may hold values from -6 to 6
Outputs:
- output: bfloat16 [4096, 1024], P('seq', 'head')
- grad_queries: bfloat16 [4096, 1024], P('seq', 'head')
- grad_keys: bfloat16 [4096, 1024], P('seq', 'head')
- grad_values: bfloat16 [4096, 1024], P('seq', 'head')
- grad_gain: float32 [1024], P('head')
The draws below stay inside these ranges and needn't reach their ends.
All inputs are finite; a program needn't handle non-finite values.
Results may differ from the reference program's by a relative error of at most 0.0044.
Values sent between devices are 32-bit elements; how exact they have to be, the bound alone decides.
A program may use at most 64 MiB of HBM per device.

```python
import math
import jax
import jax.numpy as jnp
from jax import lax

HEADS = 8
D = 128
TOK_DEV = 512
CG_STEPS = 6
TOKENS = 4096


def draw_keys(key, part):
    first, second = jax.random.split(jax.random.fold_in(key, 17))
    scales = jnp.exp(jax.random.uniform(first, (HEADS * D,), jnp.float32, math.log(0.05), 0.0))
    noise = jnp.clip(jax.random.normal(second, (TOKENS, HEADS * D), jnp.float32), -5.0, 5.0)
    return (noise * scales[None, :]).astype(jnp.bfloat16)


def level_of(stream_key, dims, cuts, least, top_value):
    def one(dim, parts):
        steps = jax.random.uniform(jax.random.fold_in(jax.random.fold_in(stream_key, 6), dim), (parts,), jnp.float32, least / len(cuts), top_value / len(cuts))
        return jnp.repeat(jnp.exp(steps), dims[dim] // parts).reshape((-1,) + (1,) * (len(dims) - dim - 1))

    loudness = one(*cuts[0])
    for cut in cuts[1:]:
        loudness = loudness * one(*cut)
    return loudness


def scatter_about(own_key, dims, deviation, limit, pieces=(), held_as=jnp.bfloat16):
    level = level_of(own_key, dims, pieces, -0.22, 0.18) if pieces else 1.0
    drawn = jax.random.normal(own_key, dims, jnp.float32) * deviation * level
    return jnp.minimum(jnp.maximum(drawn, -limit), limit).astype(held_as)


def setup_inputs(seed: int = 0) -> dict:
    arg_keys = jax.random.split(jax.random.key(seed), 7)
    queries = scatter_about(arg_keys[0], (TOKENS, HEADS * D), 1.0, 6.0, ((0, 8), (1, 4)))
    keys = draw_keys(jax.random.fold_in(arg_keys[6], 71), 0)
    values = scatter_about(arg_keys[2], (TOKENS, HEADS * D), 1.0, 6.0, ((0, 8), (1, 4)))
    ridge = jnp.clip(jnp.exp(math.log(4.0) - 2.0794415 * jax.random.uniform(arg_keys[3], (HEADS,), jnp.float32) ** level_of(arg_keys[3], (HEADS,), ((0, 4),), -0.2, 0.2)), 0.5, 4.0)
    gain = jnp.clip(1.0 + 0.1 * jax.random.normal(arg_keys[4], (HEADS * D,), jnp.float32), 0.5, 1.5)
    grad_out = scatter_about(arg_keys[5], (TOKENS, HEADS * D), 1.0, 6.0, ((0, 8), (1, 4)))
    return dict(queries=queries, keys=keys, values=values, ridge=ridge, gain=gain, grad_out=grad_out)


EPS = 1e-06
HIGH = lax.Precision.HIGHEST

def matmul(left, right):
    return jnp.dot(left, right, precision=HIGH)

def rows_by_rows(left, right):
    return lax.dot_general(left, right, (((1,), (1,)), ((), ())), precision=HIGH)

def cols_by_cols(left, right):
    return lax.dot_general(left, right, (((0,), (0,)), ((), ())), precision=HIGH)

def lower_mask(count):
    rows = lax.broadcasted_iota(jnp.int32, (count, count), 0)
    cols = lax.broadcasted_iota(jnp.int32, (count, count), 1)
    return (rows >= cols).astype(jnp.float32)

def conjugate(apply_fn, rhs):
    solution = jnp.zeros_like(rhs)
    resid = rhs
    search = rhs
    norm_now = lax.optimization_barrier(jnp.sum(resid * resid, axis=-1, keepdims=True))
    for _ in range(CG_STEPS):
        image = apply_fn(search)
        alpha = norm_now / (lax.optimization_barrier(jnp.sum(search * image, axis=-1, keepdims=True)) + EPS)
        solution = solution + alpha * search
        resid = resid - alpha * image
        norm_next = lax.optimization_barrier(jnp.sum(resid * resid, axis=-1, keepdims=True))
        search = resid + norm_next / (norm_now + EPS) * search
        norm_now = norm_next
    return solution

def make_apply(gram_prev, keys_blk, ridge, mask):

    def apply_fn(search):
        return matmul(search, gram_prev) + matmul(mask * rows_by_rows(search, keys_blk), keys_blk) + ridge * search
    return apply_fn

def forward_block(queries_blk, keys_blk, values_blk, gram_prev, assoc_prev, ridge):
    mask = lower_mask(queries_blk.shape[0])
    solved = conjugate(make_apply(gram_prev, keys_blk, ridge, mask), queries_blk)
    mixed = rows_by_rows(solved, assoc_prev) + matmul(mask * rows_by_rows(solved, keys_blk), values_blk)
    return (solved, mixed)

def adjoint_block(keys_blk, values_blk, gram_prev, assoc_prev, ridge, solved, grad_mixed):
    mask = lower_mask(keys_blk.shape[0])
    rhs = matmul(grad_mixed, assoc_prev) + matmul(mask * rows_by_rows(grad_mixed, values_blk), keys_blk)
    adjoint = conjugate(make_apply(gram_prev, keys_blk, ridge, mask), rhs)
    suffix_loc = cols_by_cols(grad_mixed, solved)
    pair = cols_by_cols(adjoint, solved)
    return (adjoint, suffix_loc, pair + pair.T)

def grads_block(keys_blk, values_blk, solved, adjoint, grad_mixed, suffix_next, pairs_next):
    upper = lower_mask(keys_blk.shape[0]).T
    key_solved = upper * rows_by_rows(keys_blk, solved)
    grad_values = rows_by_rows(keys_blk, suffix_next) + matmul(key_solved, grad_mixed)
    grad_keys = matmul(values_blk, suffix_next) + matmul(upper * rows_by_rows(values_blk, grad_mixed), solved) - matmul(keys_blk, pairs_next) - matmul(key_solved, adjoint) - matmul(upper * rows_by_rows(keys_blk, adjoint), solved)
    return (grad_keys, grad_values)

def to_heads(array):
    blocks = TOKENS // TOK_DEV
    return jnp.transpose(array.astype(jnp.float32).reshape(TOKENS, HEADS, D), (1, 0, 2)).reshape(HEADS, blocks, TOK_DEV, D)

def from_heads(array):
    return jnp.transpose(array.reshape(HEADS, TOKENS, D), (1, 0, 2)).reshape(TOKENS, HEADS * D)

def reference(queries, keys, values, ridge, gain, grad_out):
    query_h = to_heads(queries)
    key_h = to_heads(keys)
    value_h = to_heads(values)
    zeros = jnp.zeros((D, D), jnp.float32)

    def forward_head(items):
        query_b, key_b, value_b, ridge_one = items

        def step_fn(carry, blk):
            gram, assoc = carry
            query_blk, key_blk, value_blk = blk
            solved, mixed = forward_block(query_blk, key_blk, value_blk, gram, assoc, ridge_one)
            new = (gram + cols_by_cols(key_blk, key_blk), assoc + cols_by_cols(value_blk, key_blk))
            return (new, (solved, mixed, gram, assoc))
        _, outs = lax.scan(step_fn, (zeros, zeros), (query_b, key_b, value_b))
        return outs
    solved, mixed, grams, assocs = lax.map(forward_head, (query_h, key_h, value_h, ridge))
    squares = lax.optimization_barrier(jnp.sum(mixed * mixed, axis=(0, 3)))
    denom = jnp.sqrt(squares / (HEADS * D) + EPS)[None, :, :, None]
    gains = gain.reshape(HEADS, 1, 1, D)
    output = from_heads(mixed * gains / denom).astype(jnp.bfloat16)
    upstream = to_heads(grad_out)
    grad_gain = lax.optimization_barrier(jnp.sum(upstream * mixed / denom, axis=(1, 2))).reshape(HEADS * D)
    centre = lax.optimization_barrier(jnp.sum(gains * upstream * mixed, axis=(0, 3)))[None, :, :, None]
    grad_mixed = gains * upstream / denom - mixed * centre / (denom ** 3 * (HEADS * D))

    def backward_head(items):
        key_b, value_b, gram_b, assoc_b, ridge_one, solved_b, grad_b = items

        def step_fn(carry, blk):
            suffix_next, pairs_next = carry
            key_blk, value_blk, gram, assoc, solved_blk, grad_blk = blk
            adjoint, suffix_loc, pair_loc = adjoint_block(key_blk, value_blk, gram, assoc, ridge_one, solved_blk, grad_blk)
            grad_keys, grad_values = grads_block(key_blk, value_blk, solved_blk, adjoint, grad_blk, suffix_next, pairs_next)
            return ((suffix_next + suffix_loc, pairs_next + pair_loc), (adjoint, grad_keys, grad_values))
        _, outs = lax.scan(step_fn, (zeros, zeros), (key_b, value_b, gram_b, assoc_b, solved_b, grad_b), reverse=True)
        return outs
    adjoint, grad_keys, grad_values = lax.map(backward_head, (key_h, value_h, grams, assocs, ridge, solved, grad_mixed))
    return (output, from_heads(adjoint).astype(jnp.bfloat16), from_heads(grad_keys).astype(jnp.bfloat16), from_heads(grad_values).astype(jnp.bfloat16), grad_gain)
```

```python
import functools

import jax
import jax.numpy as jnp
from jax import lax
from jax.experimental import pallas as pl
from jax.experimental.pallas import tpu as pltpu
from jax.sharding import PartitionSpec as P

D = 128
CG_STEPS = 6
EPS = 1e-06
BLOCK_ROWS = 256
MESH = pl.DeviceIdType.MESH
F32 = jnp.float32
BF16 = jnp.bfloat16


def split(x):
    high = x.astype(BF16)
    return high, (x - high.astype(F32)).astype(BF16)


def dot(left, right):
    return jnp.dot(left, right, preferred_element_type=F32)


def dot_rows(left, right):
    return lax.dot_general(left, right, (((1,), (1,)), ((), ())), preferred_element_type=F32)


def side(pair):
    return jnp.concatenate(pair, axis=1)


def dot3(left, right):
    return dot(left[0], right[0]) + dot(left[1], right[0]) + dot(left[0], right[1])


def iotas(rows, cols):
    return (
        lax.broadcasted_iota(jnp.int32, (rows, cols), 0),
        lax.broadcasted_iota(jnp.int32, (rows, cols), 1),
    )


class Scan:
    def __init__(self, n, send, recv, excl, ssem, rsem, later):
        self.rounds = send.shape[0]
        self.send, self.recv, self.excl = send, recv, excl
        self.ssem, self.rsem, self.later = ssem, rsem, later
        self.me = lax.axis_index("seq")

    def partner(self, r):
        dist = 2**r
        bit = lax.rem(lax.div(self.me, dist), 2)
        return self.me + dist * (1 - 2 * bit), bit

    def copy(self, r):
        return pltpu.make_async_remote_copy(
            src_ref=self.send.at[r],
            dst_ref=self.recv.at[r],
            send_sem=self.ssem.at[r],
            recv_sem=self.rsem.at[r],
            device_id={"seq": self.partner(r)[0]},
            device_id_type=MESH,
        )

    def start(self, r):
        self.copy(r).start()

    def finish(self, r):
        self.copy(r).wait()
        _, bit = self.partner(r)
        weight = (1 - bit if self.later else bit).astype(F32)
        got = self.recv[r]
        part = weight * got
        self.excl[...] = part if r == 0 else self.excl[...] + part
        if r + 1 < self.rounds:
            self.send[r + 1] = self.send[r] + got
            self.start(r + 1)

    def total(self):
        return self.send[self.rounds - 1] + self.recv[self.rounds - 1]


def pack_sym(mats):
    if len(mats) % 2:
        return mats
    rows, cols = iotas(D, D)
    out = []
    for a, b in zip(mats[::2], mats[1::2]):
        out.append(jnp.where(rows < cols, a, b))
        diag = jnp.sum(jnp.where(rows == cols, a, 0.0), axis=0, keepdims=True)
        out.append(jnp.broadcast_to(diag, (8, D)))
    return out


def unpack_sym(ref, heads):
    if heads % 2:
        return [ref[pl.ds(h * D, D), :] for h in range(heads)]
    rows, cols = iotas(D, D)
    out = []
    for i in range(heads // 2):
        packed = ref[pl.ds(i * (D + 8), D), :]
        diag = ref[pl.ds(i * (D + 8) + D, 8), :][0:1, :]
        turned = packed.T
        a = jnp.where(rows == cols, diag, jnp.where(rows < cols, packed, turned))
        b = jnp.where(rows >= cols, packed, turned)
        out += [a, b]
    return out


def sym_rows(heads):
    return heads * D if heads % 2 else (heads // 2) * (D + 8)


def put(ref, parts):
    at = 0
    for part in parts:
        ref[0, pl.ds(at, part.shape[0]), :] = part
        at += part.shape[0]


def kernel(
    n_seq, n_head, heads, tok,
    q_ref, k_ref, v_ref, ridge_ref, gain_ref, up_ref,
    out_ref, gq_ref, gk_ref, gv_ref, gg_ref,
    kt2, vt2, k2, gram_h, gram_l,
    x_s, r_s, p_s, n_s, solved, mixed, gmix, gk_loc, gv_loc,
    gs, gr, ge, as_, ar, ae, ss, sr, se, ps, pr, pe,
    hs, hr,
    sem_s, sem_r, hsem_s, hsem_r,
):
    rows_blk = BLOCK_ROWS
    blocks = tok // rows_blk
    chains = [(h, b) for h in range(heads) for b in range(blocks)]
    scan_g = Scan(n_seq, gs, gr, ge, sem_s.at[0], sem_r.at[0], False)
    scan_a = Scan(n_seq, as_, ar, ae, sem_s.at[1], sem_r.at[1], False)
    scan_s = Scan(n_seq, ss, sr, se, sem_s.at[2], sem_r.at[2], True)
    scan_p = Scan(n_seq, ps, pr, pe, sem_s.at[3], sem_r.at[3], True)
    rounds = scan_g.rounds
    my_head = lax.axis_index("head")

    barrier = pltpu.get_barrier_semaphore()
    for r in range(rounds):
        pl.semaphore_signal(barrier, inc=1, device_id={"seq": scan_g.partner(r)[0]}, device_id_type=MESH)
    for j in range(1, n_head):
        pl.semaphore_signal(
            barrier, inc=1, device_id={"head": lax.rem(my_head + j, n_head)}, device_id_type=MESH
        )

    def tile(h, b):
        return (pl.ds(b * rows_blk, rows_blk), pl.ds(h * D, D))

    gram_blk, assoc_blk = {}, {}
    for c, (h, b) in enumerate(chains):
        key = k_ref[tile(h, b)]
        value = v_ref[tile(h, b)]
        key_t = key.astype(F32).T.astype(BF16)
        value_t = value.astype(F32).T.astype(BF16)
        kt2[c] = jnp.concatenate([key_t, key_t], axis=0)
        vt2[c] = jnp.concatenate([value_t, value_t], axis=0)
        k2[c] = side([key, key])
        both = dot(key_t, side([key, value]))
        gram_blk[h, b], assoc_blk[h, b] = both[:, :D], both[:, D:]
    put(gs, pack_sym([sum(gram_blk[h, b] for b in range(blocks)) for h in range(heads)]))
    pl.semaphore_wait(barrier, rounds + n_head - 1)
    scan_g.start(0)
    put(as_, [sum(assoc_blk[h, b] for b in range(blocks)) for h in range(heads)])

    def start_cg(c, rhs):
        x_s[c] = jnp.zeros_like(rhs)
        r_s[c] = rhs
        p_s[c] = rhs
        n_s[c] = jnp.broadcast_to(jnp.sum(rhs * rhs, axis=-1, keepdims=True), rhs.shape)

    for c, (h, b) in enumerate(chains):
        start_cg(c, q_ref[tile(h, b)].astype(F32))
    for r in range(rounds):
        scan_g.finish(r)
    scan_a.start(0)
    grams = unpack_sym(ge, heads)
    for h in range(heads):
        run = grams[h]
        for b in range(blocks):
            high, low = split(run)
            c = h * blocks + b
            gram_h[c] = jnp.concatenate([high, high], axis=0)
            gram_l[c] = low
            run = run + gram_blk[h, b]

    ri, ci = iotas(rows_blk, rows_blk)
    lower = ri >= ci
    upper = ri <= ci

    def cg_step(c, h, b):
        p = p_s[c]
        pair = split(p)
        p2 = side(pair)
        key = k_ref[tile(h, b)]
        score = split(jnp.where(lower, dot(p2, kt2[c]), 0.0))
        image = (
            dot(p2, gram_h[c]) + dot(pair[0], gram_l[c])
            + dot(score[0], key) + dot(score[1], key) + ridge_ref[h] * p
        )
        now = n_s[c]
        alpha = now / (jnp.sum(p * image, axis=-1, keepdims=True) + EPS)
        x_s[c] = x_s[c] + alpha * p
        res = r_s[c] - alpha * image
        new = jnp.broadcast_to(jnp.sum(res * res, axis=-1, keepdims=True), p.shape)
        r_s[c] = res
        n_s[c] = new
        p_s[c] = res + new / (now + EPS) * p

    spacing = max(CG_STEPS // rounds, 1)

    def solve(scan):
        def step_fn(step, carry):
            for c, (h, b) in enumerate(chains):
                cg_step(c, h, b)
            for r in range(rounds):
                if spacing * (r + 1) <= CG_STEPS:

                    @pl.when(step == spacing * (r + 1) - 1)
                    def _():
                        scan.finish(r)

            return carry

        lax.fori_loop(0, CG_STEPS, step_fn, 0)
        for r in range(rounds):
            if spacing * (r + 1) > CG_STEPS:
                scan.finish(r)

    solve(scan_a)

    assoc_all = {}
    for h in range(heads):
        run = ae[pl.ds(h * D, D), :]
        for b in range(blocks):
            c = h * blocks + b
            assoc_all[h, b] = run
            x = x_s[c]
            solved[c] = x
            pair = split(x)
            value = v_ref[tile(h, b)]
            score = split(jnp.where(lower, dot(side(pair), kt2[c]), 0.0))
            mixed[c] = dot3(pair, split(run)) + dot(score[0], value) + dot(score[1], value)
            run = run + assoc_blk[h, b]

    ones = jnp.ones((16, D), BF16)
    for b in range(blocks):
        square = jnp.zeros((16, rows_blk), F32)
        centre = jnp.zeros((16, rows_blk), F32)
        for h in range(heads):
            m = mixed[h * blocks + b]
            gain = gain_ref[:, pl.ds(h * D, D)]
            up = up_ref[tile(h, b)].astype(F32)
            for part in split(m * m):
                square = square + dot_rows(ones, part)
            for part in split(gain * up * m):
                centre = centre + dot_rows(ones, part)
        row, _ = iotas(8, rows_blk)
        hs[:, pl.ds(b * rows_blk, rows_blk)] = jnp.where(row < 4, square[:8], centre[:8])

    def head_copy(j):
        return pltpu.make_async_remote_copy(
            src_ref=hs,
            dst_ref=hr.at[j - 1],
            send_sem=hsem_s.at[j - 1],
            recv_sem=hsem_r.at[j - 1],
            device_id={"head": lax.rem(my_head + j, n_head)},
            device_id_type=MESH,
        )

    for j in range(1, n_head):
        head_copy(j).start()
    for j in range(1, n_head):
        head_copy(j).wait()
    sums = hs[...]
    for j in range(1, n_head):
        sums = sums + hr[j - 1]
    width = n_head * heads * D
    gain_rows = [jnp.zeros((8, D), F32) for _ in range(heads)]
    suffix_blk = {}
    for b in range(blocks):
        sums_t = jnp.concatenate([sums[:, b * rows_blk:(b + 1) * rows_blk]] * 16, axis=0).T
        denom = jnp.sqrt(sums_t[:, 0:1] / width + EPS)
        inv = 1.0 / denom
        factor = sums_t[:, 4:5] / (denom * denom * denom * width)
        inv = jnp.broadcast_to(inv, (rows_blk, D))
        factor = jnp.broadcast_to(factor, (rows_blk, D))
        for h in range(heads):
            c = h * blocks + b
            m = mixed[c]
            gain = gain_ref[:, pl.ds(h * D, D)]
            up = up_ref[tile(h, b)].astype(F32)
            normed = m * inv
            out_ref[tile(h, b)] = (normed * gain).astype(BF16)
            gain_rows[h] = gain_rows[h] + jnp.sum((up * normed).reshape(rows_blk // 8, 8, D), axis=0)
            grad = gain * up * inv - m * factor
            gmix[c] = grad
            suffix_blk[h, b] = dot3(split(grad.T), split(solved[c]))
    put(ss, [sum(suffix_blk[h, b] for b in range(blocks)) for h in range(heads)] + gain_rows)
    scan_s.start(0)

    for c, (h, b) in enumerate(chains):
        key = k_ref[tile(h, b)]
        pair = split(gmix[c])
        score = split(jnp.where(lower, dot(side(pair), vt2[c]), 0.0))
        rhs = dot3(pair, split(assoc_all[h, b].T)) + dot(score[0], key) + dot(score[1], key)
        start_cg(c, rhs)
    solve(scan_s)

    pair_blk = {}
    for c, (h, b) in enumerate(chains):
        adj = x_s[c]
        gq_ref[tile(h, b)] = adj.astype(BF16)
        one = dot3(split(adj.T), split(solved[c]))
        pair_blk[h, b] = one + one.T
    put(ps, pack_sym([sum(pair_blk[h, b] for b in range(blocks)) for h in range(heads)]))
    scan_p.start(0)

    gain_total = scan_s.total()
    for h in range(heads):
        rows = gain_total[heads * D + 8 * h:heads * D + 8 * h + 8, :]
        gg_ref[:, pl.ds(h * D, D)] = jnp.sum(rows, axis=0, keepdims=True)

    done = 0
    for h in range(heads):
        run = se[pl.ds(h * D, D), :]
        for b in reversed(range(blocks)):
            c = h * blocks + b
            key = k_ref[tile(h, b)]
            value = v_ref[tile(h, b)]
            sol, adj, grad = split(solved[c]), split(x_s[c]), split(gmix[c])
            key_sol = split(jnp.where(upper, dot_rows(k2[c], side(sol)), 0.0))
            cross = split(jnp.where(
                upper,
                dot_rows(side([value, value]), side(grad)) - dot_rows(k2[c], side(adj)),
                0.0,
            ))
            suf = split(run)
            suf_t = split(run.T)
            gv = dot(key, suf_t[0]) + dot(key, suf_t[1]) + dot3(key_sol, grad)
            gv_ref[tile(h, b)] = gv.astype(BF16)
            gk_loc[c] = (
                dot(value, suf[0]) + dot(value, suf[1]) + dot3(cross, sol) - dot3(key_sol, adj)
            )
            run = run + suffix_blk[h, b]
            if done < rounds:
                scan_p.finish(done)
                done += 1
    while done < rounds:
        scan_p.finish(done)
        done += 1
    pairs = unpack_sym(pe, heads)
    for h in range(heads):
        run = pairs[h]
        for b in reversed(range(blocks)):
            c = h * blocks + b
            key = k_ref[tile(h, b)]
            high, low = split(run)
            gk_ref[tile(h, b)] = (gk_loc[c] - dot(key, high) - dot(key, low)).astype(BF16)
            run = run + pair_blk[h, b]


def per_device(n_seq, n_head, queries, keys, values, ridge, gain, grad_out):
    tok = queries.shape[0]
    heads = ridge.shape[0]
    rounds = n_seq.bit_length() - 1
    chains = heads * (tok // BLOCK_ROWS)
    rows = BLOCK_ROWS
    sym = sym_rows(heads)
    suf = heads * (D + 8)
    vm = pltpu.VMEM

    def state(count):
        return [vm((rounds, count, D), F32), vm((rounds, count, D), F32), vm((count, D), F32)]

    big = [vm((chains, rows, D), F32)] * 9
    wide = jax.ShapeDtypeStruct((tok, heads * D), BF16)
    spec = pl.BlockSpec(memory_space=pltpu.VMEM)
    outs = pl.pallas_call(
        functools.partial(kernel, n_seq, n_head, heads, tok),
        out_shape=[wide, wide, wide, wide, jax.ShapeDtypeStruct((1, heads * D), F32)],
        in_specs=[spec, spec, spec, pl.BlockSpec(memory_space=pltpu.SMEM), spec, spec],
        out_specs=[spec] * 5,
        scratch_shapes=[
            vm((chains, 2 * D, rows), BF16),
            vm((chains, 2 * D, rows), BF16),
            vm((chains, rows, 2 * D), BF16),
            vm((chains, 2 * D, D), BF16),
            vm((chains, D, D), BF16),
        ]
        + big
        + state(sym) + state(heads * D) + state(suf) + state(sym)
        + [
            vm((8, tok), F32),
            vm((n_head - 1, 8, tok), F32),
            pltpu.SemaphoreType.DMA((4, rounds)),
            pltpu.SemaphoreType.DMA((4, rounds)),
            pltpu.SemaphoreType.DMA((n_head - 1,)),
            pltpu.SemaphoreType.DMA((n_head - 1,)),
        ],
        compiler_params=pltpu.CompilerParams(
            collective_id=0, has_side_effects=True, vmem_limit_bytes=40 * 2**20
        ),
    )(queries, keys, values, ridge, gain.reshape(1, -1), grad_out)
    return (*outs[:4], outs[4].reshape(-1))


def solution(mesh):
    n_seq, n_head = mesh.shape["seq"], mesh.shape["head"]
    wide = P("seq", "head")
    return jax.shard_map(
        functools.partial(per_device, n_seq, n_head),
        mesh=mesh,
        in_specs=(wide, wide, wide, P("head"), P("head"), wide),
        out_specs=(wide, wide, wide, wide, P("head")),
        check_vma=False,
    )
```

```python
import functools

import jax
import jax.numpy as jnp
from jax import lax
from jax.experimental import pallas as pl
from jax.experimental.pallas import tpu as pltpu
from jax.sharding import PartitionSpec as P

D = 128
CG_STEPS = 6
EPS = 1e-06
BLOCK_ROWS = 256
MESH = pl.DeviceIdType.MESH
F32 = jnp.float32
BF16 = jnp.bfloat16


def split(x):
    high = x.astype(BF16)
    return high, (x - high.astype(F32)).astype(BF16)


def dot(left, right):
    return jnp.dot(left, right, preferred_element_type=F32)


def dot_rows(left, right):
    return lax.dot_general(left, right, (((1,), (1,)), ((), ())), preferred_element_type=F32)


def side(pair):
    return jnp.concatenate(pair, axis=1)


def dot3(left, right):
    return dot(left[0], right[0]) + dot(left[1], right[0]) + dot(left[0], right[1])


def iotas(rows, cols):
    return (
        lax.broadcasted_iota(jnp.int32, (rows, cols), 0),
        lax.broadcasted_iota(jnp.int32, (rows, cols), 1),
    )


class Scan:
    def __init__(self, n, send, recv, excl, ssem, rsem, later):
        self.rounds = send.shape[0]
        self.send, self.recv, self.excl = send, recv, excl
        self.ssem, self.rsem, self.later = ssem, rsem, later
        self.me = lax.axis_index("seq")

    def partner(self, r):
        dist = 2**r
        bit = lax.rem(lax.div(self.me, dist), 2)
        return self.me + dist * (1 - 2 * bit), bit

    def copy(self, r):
        return pltpu.make_async_remote_copy(
            src_ref=self.send.at[r],
            dst_ref=self.recv.at[r],
            send_sem=self.ssem.at[r],
            recv_sem=self.rsem.at[r],
            device_id={"seq": self.partner(r)[0]},
            device_id_type=MESH,
        )

    def start(self, r):
        self.copy(r).start()

    def finish(self, r):
        self.copy(r).wait()
        _, bit = self.partner(r)
        weight = (1 - bit if self.later else bit).astype(F32)
        got = self.recv[r]
        part = weight * got
        self.excl[...] = part if r == 0 else self.excl[...] + part
        if r + 1 < self.rounds:
            self.send[r + 1] = self.send[r] + got
            self.start(r + 1)

    def total(self):
        return self.send[self.rounds - 1] + self.recv[self.rounds - 1]


def pack_sym(mats):
    if len(mats) % 2:
        return mats
    rows, cols = iotas(D, D)
    out = []
    for a, b in zip(mats[::2], mats[1::2]):
        out.append(jnp.where(rows < cols, a, b))
        diag = jnp.sum(jnp.where(rows == cols, a, 0.0), axis=0, keepdims=True)
        out.append(jnp.broadcast_to(diag, (8, D)))
    return out


def unpack_sym(ref, heads):
    if heads % 2:
        return [ref[pl.ds(h * D, D), :] for h in range(heads)]
    rows, cols = iotas(D, D)
    out = []
    for i in range(heads // 2):
        packed = ref[pl.ds(i * (D + 8), D), :]
        diag = ref[pl.ds(i * (D + 8) + D, 8), :][0:1, :]
        turned = packed.T
        a = jnp.where(rows == cols, diag, jnp.where(rows < cols, packed, turned))
        b = jnp.where(rows >= cols, packed, turned)
        out += [a, b]
    return out


def sym_rows(heads):
    return heads * D if heads % 2 else (heads // 2) * (D + 8)


def put(ref, parts):
    at = 0
    for part in parts:
        ref[0, pl.ds(at, part.shape[0]), :] = part
        at += part.shape[0]


def kernel(
    n_seq, n_head, heads, tok,
    q_hbm, k_hbm, v_hbm, ridge_ref, gain_ref, up_hbm,
    out_ref, gq_ref, gk_ref, gv_ref, gg_ref,
    q_ref, k_ref, v_ref, up_ref,
    kt2, vt2, k2, gram_h, gram_l,
    x_s, r_s, p_s, n_s, solved, mixed, gmix, gk_loc, gv_loc,
    gs, gr, ge, as_, ar, ae, ss, sr, se, ps, pr, pe,
    hs, hr,
    sem_s, sem_r, hsem_s, hsem_r, in_sem,
):
    loads = [
        pltpu.make_async_copy(src, dst, in_sem.at[i])
        for i, (src, dst) in enumerate(
            [(k_hbm, k_ref), (v_hbm, v_ref), (q_hbm, q_ref), (up_hbm, up_ref)]
        )
    ]
    for load in loads:
        load.start()
    rows_blk = BLOCK_ROWS
    blocks = tok // rows_blk
    chains = [(h, b) for h in range(heads) for b in range(blocks)]
    scan_g = Scan(n_seq, gs, gr, ge, sem_s.at[0], sem_r.at[0], False)
    scan_a = Scan(n_seq, as_, ar, ae, sem_s.at[1], sem_r.at[1], False)
    scan_s = Scan(n_seq, ss, sr, se, sem_s.at[2], sem_r.at[2], True)
    scan_p = Scan(n_seq, ps, pr, pe, sem_s.at[3], sem_r.at[3], True)
    rounds = scan_g.rounds
    my_head = lax.axis_index("head")

    barrier = pltpu.get_barrier_semaphore()
    for r in range(rounds):
        pl.semaphore_signal(barrier, inc=1, device_id={"seq": scan_g.partner(r)[0]}, device_id_type=MESH)
    for j in range(1, n_head):
        pl.semaphore_signal(
            barrier, inc=1, device_id={"head": lax.rem(my_head + j, n_head)}, device_id_type=MESH
        )

    def tile(h, b):
        return (pl.ds(b * rows_blk, rows_blk), pl.ds(h * D, D))

    loads[0].wait()
    loads[1].wait()
    gram_blk, assoc_blk = {}, {}
    for c, (h, b) in enumerate(chains):
        key = k_ref[tile(h, b)]
        value = v_ref[tile(h, b)]
        key_t = key.astype(F32).T.astype(BF16)
        value_t = value.astype(F32).T.astype(BF16)
        kt2[c] = jnp.concatenate([key_t, key_t], axis=0)
        vt2[c] = jnp.concatenate([value_t, value_t], axis=0)
        k2[c] = side([key, key])
        both = dot(key_t, side([key, value]))
        gram_blk[h, b], assoc_blk[h, b] = both[:, :D], both[:, D:]
    put(gs, pack_sym([sum(gram_blk[h, b] for b in range(blocks)) for h in range(heads)]))
    pl.semaphore_wait(barrier, rounds + n_head - 1)
    scan_g.start(0)
    put(as_, [sum(assoc_blk[h, b] for b in range(blocks)) for h in range(heads)])

    def start_cg(c, rhs):
        x_s[c] = jnp.zeros_like(rhs)
        r_s[c] = rhs
        p_s[c] = rhs
        n_s[c] = jnp.broadcast_to(jnp.sum(rhs * rhs, axis=-1, keepdims=True), rhs.shape)

    loads[2].wait()
    for c, (h, b) in enumerate(chains):
        start_cg(c, q_ref[tile(h, b)].astype(F32))
    for r in range(rounds):
        scan_g.finish(r)
    scan_a.start(0)
    grams = unpack_sym(ge, heads)
    for h in range(heads):
        run = grams[h]
        for b in range(blocks):
            high, low = split(run)
            c = h * blocks + b
            gram_h[c] = jnp.concatenate([high, high], axis=0)
            gram_l[c] = low
            run = run + gram_blk[h, b]

    ri, ci = iotas(rows_blk, rows_blk)
    lower = ri >= ci
    upper = ri <= ci

    def cg_step(c, h, b):
        p = p_s[c]
        pair = split(p)
        p2 = side(pair)
        key = k_ref[tile(h, b)]
        score = split(jnp.where(lower, dot(p2, kt2[c]), 0.0))
        image = (
            dot(p2, gram_h[c]) + dot(pair[0], gram_l[c])
            + dot(score[0], key) + dot(score[1], key) + ridge_ref[h] * p
        )
        now = n_s[c]
        alpha = now / (jnp.sum(p * image, axis=-1, keepdims=True) + EPS)
        x_s[c] = x_s[c] + alpha * p
        res = r_s[c] - alpha * image
        new = jnp.broadcast_to(jnp.sum(res * res, axis=-1, keepdims=True), p.shape)
        r_s[c] = res
        n_s[c] = new
        p_s[c] = res + new / (now + EPS) * p

    spacing = max(CG_STEPS // rounds, 1)

    def solve(scan):
        def step_fn(step, carry):
            for c, (h, b) in enumerate(chains):
                cg_step(c, h, b)
            for r in range(rounds):
                if spacing * (r + 1) <= CG_STEPS:

                    @pl.when(step == spacing * (r + 1) - 1)
                    def _():
                        scan.finish(r)

            return carry

        lax.fori_loop(0, CG_STEPS, step_fn, 0)
        for r in range(rounds):
            if spacing * (r + 1) > CG_STEPS:
                scan.finish(r)

    solve(scan_a)
    loads[3].wait()

    assoc_all = {}
    for h in range(heads):
        run = ae[pl.ds(h * D, D), :]
        for b in range(blocks):
            c = h * blocks + b
            assoc_all[h, b] = run
            x = x_s[c]
            solved[c] = x
            pair = split(x)
            value = v_ref[tile(h, b)]
            score = split(jnp.where(lower, dot(side(pair), kt2[c]), 0.0))
            mixed[c] = dot3(pair, split(run)) + dot(score[0], value) + dot(score[1], value)
            run = run + assoc_blk[h, b]

    ones = jnp.ones((16, D), BF16)
    for b in range(blocks):
        square = jnp.zeros((16, rows_blk), F32)
        centre = jnp.zeros((16, rows_blk), F32)
        for h in range(heads):
            m = mixed[h * blocks + b]
            gain = gain_ref[:, pl.ds(h * D, D)]
            up = up_ref[tile(h, b)].astype(F32)
            for part in split(m * m):
                square = square + dot_rows(ones, part)
            for part in split(gain * up * m):
                centre = centre + dot_rows(ones, part)
        row, _ = iotas(8, rows_blk)
        hs[:, pl.ds(b * rows_blk, rows_blk)] = jnp.where(row < 4, square[:8], centre[:8])

    def head_copy(j):
        return pltpu.make_async_remote_copy(
            src_ref=hs,
            dst_ref=hr.at[j - 1],
            send_sem=hsem_s.at[j - 1],
            recv_sem=hsem_r.at[j - 1],
            device_id={"head": lax.rem(my_head + j, n_head)},
            device_id_type=MESH,
        )

    for j in range(1, n_head):
        head_copy(j).start()
    for j in range(1, n_head):
        head_copy(j).wait()
    sums = hs[...]
    for j in range(1, n_head):
        sums = sums + hr[j - 1]
    width = n_head * heads * D
    gain_rows = [jnp.zeros((8, D), F32) for _ in range(heads)]
    suffix_blk = {}
    for b in range(blocks):
        sums_t = jnp.concatenate([sums[:, b * rows_blk:(b + 1) * rows_blk]] * 16, axis=0).T
        denom = jnp.sqrt(sums_t[:, 0:1] / width + EPS)
        inv = 1.0 / denom
        factor = sums_t[:, 4:5] / (denom * denom * denom * width)
        inv = jnp.broadcast_to(inv, (rows_blk, D))
        factor = jnp.broadcast_to(factor, (rows_blk, D))
        for h in range(heads):
            c = h * blocks + b
            m = mixed[c]
            gain = gain_ref[:, pl.ds(h * D, D)]
            up = up_ref[tile(h, b)].astype(F32)
            normed = m * inv
            out_ref[tile(h, b)] = (normed * gain).astype(BF16)
            gain_rows[h] = gain_rows[h] + jnp.sum((up * normed).reshape(rows_blk // 8, 8, D), axis=0)
            grad = gain * up * inv - m * factor
            gmix[c] = grad
            suffix_blk[h, b] = dot3(split(grad.T), split(solved[c]))
    put(ss, [sum(suffix_blk[h, b] for b in range(blocks)) for h in range(heads)] + gain_rows)
    scan_s.start(0)

    for c, (h, b) in enumerate(chains):
        key = k_ref[tile(h, b)]
        pair = split(gmix[c])
        score = split(jnp.where(lower, dot(side(pair), vt2[c]), 0.0))
        rhs = dot3(pair, split(assoc_all[h, b].T)) + dot(score[0], key) + dot(score[1], key)
        start_cg(c, rhs)
    solve(scan_s)

    pair_blk = {}
    for c, (h, b) in enumerate(chains):
        adj = x_s[c]
        gq_ref[tile(h, b)] = adj.astype(BF16)
        one = dot3(split(adj.T), split(solved[c]))
        pair_blk[h, b] = one + one.T
    put(ps, pack_sym([sum(pair_blk[h, b] for b in range(blocks)) for h in range(heads)]))
    scan_p.start(0)

    gain_total = scan_s.total()
    for h in range(heads):
        rows = gain_total[heads * D + 8 * h:heads * D + 8 * h + 8, :]
        gg_ref[:, pl.ds(h * D, D)] = jnp.sum(rows, axis=0, keepdims=True)

    done = 0
    for h in range(heads):
        run = se[pl.ds(h * D, D), :]
        for b in reversed(range(blocks)):
            c = h * blocks + b
            key = k_ref[tile(h, b)]
            value = v_ref[tile(h, b)]
            sol, adj, grad = split(solved[c]), split(x_s[c]), split(gmix[c])
            key_sol = split(jnp.where(upper, dot_rows(k2[c], side(sol)), 0.0))
            cross = split(jnp.where(
                upper,
                dot_rows(side([value, value]), side(grad)) - dot_rows(k2[c], side(adj)),
                0.0,
            ))
            suf = split(run)
            suf_t = split(run.T)
            gv = dot(key, suf_t[0]) + dot(key, suf_t[1]) + dot3(key_sol, grad)
            gv_ref[tile(h, b)] = gv.astype(BF16)
            gk_loc[c] = (
                dot(value, suf[0]) + dot(value, suf[1]) + dot3(cross, sol) - dot3(key_sol, adj)
            )
            run = run + suffix_blk[h, b]
            if done < rounds:
                scan_p.finish(done)
                done += 1
    while done < rounds:
        scan_p.finish(done)
        done += 1
    pairs = unpack_sym(pe, heads)
    for h in range(heads):
        run = pairs[h]
        for b in reversed(range(blocks)):
            c = h * blocks + b
            key = k_ref[tile(h, b)]
            high, low = split(run)
            gk_ref[tile(h, b)] = (gk_loc[c] - dot(key, high) - dot(key, low)).astype(BF16)
            run = run + pair_blk[h, b]


def hand_over(*refs):
    sources, targets, sem = refs[:5], refs[5:10], refs[10]
    copies = [
        pltpu.make_async_copy(src, dst, sem.at[i])
        for i, (src, dst) in enumerate(zip(sources, targets))
    ]
    for copy in copies:
        copy.start()
    for copy in copies:
        copy.wait()


def per_device(n_seq, n_head, queries, keys, values, ridge, gain, grad_out):
    tok = queries.shape[0]
    heads = ridge.shape[0]
    rounds = n_seq.bit_length() - 1
    chains = heads * (tok // BLOCK_ROWS)
    rows = BLOCK_ROWS
    sym = sym_rows(heads)
    suf = heads * (D + 8)
    vm = pltpu.VMEM

    def state(count):
        return [vm((rounds, count, D), F32), vm((rounds, count, D), F32), vm((count, D), F32)]

    big = [vm((chains, rows, D), F32)] * 9
    wide = jax.ShapeDtypeStruct((tok, heads * D), BF16)
    spec = pl.BlockSpec(memory_space=pltpu.VMEM)
    far = pl.BlockSpec(memory_space=pl.ANY)
    near = vm((tok, heads * D), BF16)
    outs = pl.pallas_call(
        functools.partial(kernel, n_seq, n_head, heads, tok),
        out_shape=[wide, wide, wide, wide, jax.ShapeDtypeStruct((1, heads * D), F32)],
        in_specs=[far, far, far, pl.BlockSpec(memory_space=pltpu.SMEM), spec, far],
        out_specs=[spec] * 5,
        scratch_shapes=[
            near, near, near, near,
            vm((chains, 2 * D, rows), BF16),
            vm((chains, 2 * D, rows), BF16),
            vm((chains, rows, 2 * D), BF16),
            vm((chains, 2 * D, D), BF16),
            vm((chains, D, D), BF16),
        ]
        + big
        + state(sym) + state(heads * D) + state(suf) + state(sym)
        + [
            vm((8, tok), F32),
            vm((n_head - 1, 8, tok), F32),
            pltpu.SemaphoreType.DMA((4, rounds)),
            pltpu.SemaphoreType.DMA((4, rounds)),
            pltpu.SemaphoreType.DMA((n_head - 1,)),
            pltpu.SemaphoreType.DMA((n_head - 1,)),
            pltpu.SemaphoreType.DMA((4,)),
        ],
        compiler_params=pltpu.CompilerParams(
            collective_id=0, has_side_effects=True, vmem_limit_bytes=63 * 2**20
        ),
    )(queries, keys, values, ridge, gain.reshape(1, -1), grad_out)
    outs = pl.pallas_call(
        hand_over,
        out_shape=[jax.ShapeDtypeStruct(x.shape, x.dtype) for x in outs],
        in_specs=[far] * 5,
        out_specs=[far] * 5,
        scratch_shapes=[pltpu.SemaphoreType.DMA((5,))],
        compiler_params=pltpu.CompilerParams(vmem_limit_bytes=63 * 2**20),
    )(*outs)
    return (*outs[:4], outs[4].reshape(-1))


def solution(mesh):
    n_seq, n_head = mesh.shape["seq"], mesh.shape["head"]
    wide = P("seq", "head")
    return jax.shard_map(
        functools.partial(per_device, n_seq, n_head),
        mesh=mesh,
        in_specs=(wide, wide, wide, P("head"), P("head"), wide),
        out_specs=(wide, wide, wide, wide, P("head")),
        check_vma=False,
    )
```

```python
import functools

import jax
import jax.numpy as jnp
from jax import lax
from jax.experimental import pallas as pl
from jax.experimental.pallas import tpu as pltpu
from jax.sharding import PartitionSpec as P

D = 128
CG_STEPS = 6
EPS = 1e-06
BLOCK_ROWS = 256
MESH = pl.DeviceIdType.MESH
F32 = jnp.float32
BF16 = jnp.bfloat16


def split(x):
    high = x.astype(BF16)
    return high, (x - high.astype(F32)).astype(BF16)


def dot(left, right):
    return jnp.dot(left, right, preferred_element_type=F32)


def dot_rows(left, right):
    return lax.dot_general(left, right, (((1,), (1,)), ((), ())), preferred_element_type=F32)


def side(pair):
    return jnp.concatenate(pair, axis=1)


def dot3(left, right):
    return dot(left[0], right[0]) + dot(left[1], right[0]) + dot(left[0], right[1])


def iotas(rows, cols):
    return (
        lax.broadcasted_iota(jnp.int32, (rows, cols), 0),
        lax.broadcasted_iota(jnp.int32, (rows, cols), 1),
    )


class Scan:
    def __init__(self, n, send, recv, excl, ssem, rsem, later):
        self.rounds = send.shape[0]
        self.send, self.recv, self.excl = send, recv, excl
        self.ssem, self.rsem, self.later = ssem, rsem, later
        self.me = lax.axis_index("seq")

    def partner(self, r):
        dist = 2**r
        bit = lax.rem(lax.div(self.me, dist), 2)
        return self.me + dist * (1 - 2 * bit), bit

    def copy(self, r):
        return pltpu.make_async_remote_copy(
            src_ref=self.send.at[r],
            dst_ref=self.recv.at[r],
            send_sem=self.ssem.at[r],
            recv_sem=self.rsem.at[r],
            device_id={"seq": self.partner(r)[0]},
            device_id_type=MESH,
        )

    def start(self, r):
        self.copy(r).start()

    def finish(self, r):
        self.copy(r).wait()
        _, bit = self.partner(r)
        weight = (1 - bit if self.later else bit).astype(F32)
        got = self.recv[r]
        part = weight * got
        self.excl[...] = part if r == 0 else self.excl[...] + part
        if r + 1 < self.rounds:
            self.send[r + 1] = self.send[r] + got
            self.start(r + 1)

    def total(self):
        return self.send[self.rounds - 1] + self.recv[self.rounds - 1]


def pack_sym(mats):
    if len(mats) % 2:
        return mats
    rows, cols = iotas(D, D)
    out = []
    for a, b in zip(mats[::2], mats[1::2]):
        out.append(jnp.where(rows < cols, a, b))
        diag = jnp.sum(jnp.where(rows == cols, a, 0.0), axis=0, keepdims=True)
        out.append(jnp.broadcast_to(diag, (8, D)))
    return out


def unpack_sym(ref, heads):
    if heads % 2:
        return [ref[pl.ds(h * D, D), :] for h in range(heads)]
    rows, cols = iotas(D, D)
    out = []
    for i in range(heads // 2):
        packed = ref[pl.ds(i * (D + 8), D), :]
        diag = ref[pl.ds(i * (D + 8) + D, 8), :][0:1, :]
        turned = packed.T
        a = jnp.where(rows == cols, diag, jnp.where(rows < cols, packed, turned))
        b = jnp.where(rows >= cols, packed, turned)
        out += [a, b]
    return out


def sym_rows(heads):
    return heads * D if heads % 2 else (heads // 2) * (D + 8)


def put(ref, parts):
    at = 0
    for part in parts:
        ref[0, pl.ds(at, part.shape[0]), :] = part
        at += part.shape[0]


def kernel(
    n_seq, n_head, heads, tok,
    q_ref, k_ref, v_ref, ridge_ref, gain_ref, up_ref,
    out_ref, gq_ref, gk_ref, gv_ref, gg_ref,
    kt2, vt2, k2, gram_h, gram_l,
    x_s, r_s, p_s, n_s, solved, mixed, gmix, gk_loc, gv_loc,
    gs, gr, ge, as_, ar, ae, ss, sr, se, ps, pr, pe,
    hs, hr,
    sem_s, sem_r, hsem_s, hsem_r,
):
    rows_blk = BLOCK_ROWS
    blocks = tok // rows_blk
    chains = [(h, b) for h in range(heads) for b in range(blocks)]
    scan_g = Scan(n_seq, gs, gr, ge, sem_s.at[0], sem_r.at[0], False)
    scan_a = Scan(n_seq, as_, ar, ae, sem_s.at[1], sem_r.at[1], False)
    scan_s = Scan(n_seq, ss, sr, se, sem_s.at[2], sem_r.at[2], True)
    scan_p = Scan(n_seq, ps, pr, pe, sem_s.at[3], sem_r.at[3], True)
    rounds = scan_g.rounds
    my_head = lax.axis_index("head")

    barrier = pltpu.get_barrier_semaphore()
    for r in range(rounds):
        pl.semaphore_signal(barrier, inc=1, device_id={"seq": scan_g.partner(r)[0]}, device_id_type=MESH)
    for j in range(1, n_head):
        pl.semaphore_signal(
            barrier, inc=1, device_id={"head": lax.rem(my_head + j, n_head)}, device_id_type=MESH
        )

    def tile(h, b):
        return (pl.ds(b * rows_blk, rows_blk), pl.ds(h * D, D))

    gram_blk, assoc_blk = {}, {}
    for c, (h, b) in enumerate(chains):
        key = k_ref[tile(h, b)]
        value = v_ref[tile(h, b)]
        key_t = key.astype(F32).T.astype(BF16)
        kt2[c] = jnp.concatenate([key_t, key_t], axis=0)
        k2[c] = side([key, key])
        both = dot(key_t, side([key, value]))
        gram_blk[h, b], assoc_blk[h, b] = both[:, :D], both[:, D:]
    put(gs, pack_sym([sum(gram_blk[h, b] for b in range(blocks)) for h in range(heads)]))
    pl.semaphore_wait(barrier, rounds + n_head - 1)
    scan_g.start(0)
    put(as_, [sum(assoc_blk[h, b] for b in range(blocks)) for h in range(heads)])

    def start_cg(c, rhs):
        x_s[c] = jnp.zeros_like(rhs)
        r_s[c] = rhs
        p_s[c] = rhs
        n_s[c] = jnp.broadcast_to(jnp.sum(rhs * rhs, axis=-1, keepdims=True), rhs.shape)

    for c, (h, b) in enumerate(chains):
        start_cg(c, q_ref[tile(h, b)].astype(F32))
        value_t = v_ref[tile(h, b)].astype(F32).T.astype(BF16)
        vt2[c] = jnp.concatenate([value_t, value_t], axis=0)
    for r in range(rounds):
        scan_g.finish(r)
    scan_a.start(0)
    grams = unpack_sym(ge, heads)
    for h in range(heads):
        run = grams[h]
        for b in range(blocks):
            high, low = split(run)
            c = h * blocks + b
            gram_h[c] = jnp.concatenate([high, high], axis=0)
            gram_l[c] = low
            run = run + gram_blk[h, b]

    ri, ci = iotas(rows_blk, rows_blk)
    lower = ri >= ci
    upper = ri <= ci

    def cg_step(c, h, b, last=False):
        p = p_s[c]
        pair = split(p)
        p2 = side(pair)
        key = k_ref[tile(h, b)]
        score = split(jnp.where(lower, dot(p2, kt2[c]), 0.0))
        image = (
            dot(p2, gram_h[c]) + dot(pair[0], gram_l[c])
            + dot(score[0], key) + dot(score[1], key) + ridge_ref[h] * p
        )
        now = n_s[c]
        alpha = now / (jnp.sum(p * image, axis=-1, keepdims=True) + EPS)
        x_s[c] = x_s[c] + alpha * p
        if last:
            return
        res = r_s[c] - alpha * image
        new = jnp.broadcast_to(jnp.sum(res * res, axis=-1, keepdims=True), p.shape)
        r_s[c] = res
        n_s[c] = new
        p_s[c] = res + new / (now + EPS) * p

    spacing = max(CG_STEPS // rounds, 1)

    def solve(scan):
        def step_fn(step, carry):
            for c, (h, b) in enumerate(chains):
                cg_step(c, h, b)
            for r in range(rounds):
                if spacing * (r + 1) < CG_STEPS:

                    @pl.when(step == spacing * (r + 1) - 1)
                    def _():
                        scan.finish(r)

            return carry

        lax.fori_loop(0, CG_STEPS - 1, step_fn, 0)
        for c, (h, b) in enumerate(chains):
            cg_step(c, h, b, last=True)
        for r in range(rounds):
            if spacing * (r + 1) >= CG_STEPS:
                scan.finish(r)

    solve(scan_a)

    assoc_all = {}
    for h in range(heads):
        run = ae[pl.ds(h * D, D), :]
        for b in range(blocks):
            c = h * blocks + b
            assoc_all[h, b] = run
            x = x_s[c]
            solved[c] = x
            pair = split(x)
            value = v_ref[tile(h, b)]
            score = split(jnp.where(lower, dot(side(pair), kt2[c]), 0.0))
            mixed[c] = dot3(pair, split(run)) + dot(score[0], value) + dot(score[1], value)
            run = run + assoc_blk[h, b]

    ones = jnp.ones((16, D), BF16)
    for b in range(blocks):
        square = jnp.zeros((16, rows_blk), F32)
        centre = jnp.zeros((16, rows_blk), F32)
        for h in range(heads):
            m = mixed[h * blocks + b]
            gain = gain_ref[:, pl.ds(h * D, D)]
            up = up_ref[tile(h, b)].astype(F32)
            for part in split(m * m):
                square = square + dot_rows(ones, part)
            for part in split(gain * up * m):
                centre = centre + dot_rows(ones, part)
        row, _ = iotas(8, rows_blk)
        hs[:, pl.ds(b * rows_blk, rows_blk)] = jnp.where(row < 4, square[:8], centre[:8])

    def head_copy(j):
        return pltpu.make_async_remote_copy(
            src_ref=hs,
            dst_ref=hr.at[j - 1],
            send_sem=hsem_s.at[j - 1],
            recv_sem=hsem_r.at[j - 1],
            device_id={"head": lax.rem(my_head + j, n_head)},
            device_id_type=MESH,
        )

    for j in range(1, n_head):
        head_copy(j).start()
    for j in range(1, n_head):
        head_copy(j).wait()
    sums = hs[...]
    for j in range(1, n_head):
        sums = sums + hr[j - 1]
    width = n_head * heads * D
    gain_rows = [jnp.zeros((8, D), F32) for _ in range(heads)]
    suffix_blk = {}
    for b in range(blocks):
        sums_t = jnp.concatenate([sums[:, b * rows_blk:(b + 1) * rows_blk]] * 16, axis=0).T
        denom = jnp.sqrt(sums_t[:, 0:1] / width + EPS)
        inv = 1.0 / denom
        factor = sums_t[:, 4:5] / (denom * denom * denom * width)
        inv = jnp.broadcast_to(inv, (rows_blk, D))
        factor = jnp.broadcast_to(factor, (rows_blk, D))
        for h in range(heads):
            c = h * blocks + b
            m = mixed[c]
            gain = gain_ref[:, pl.ds(h * D, D)]
            up = up_ref[tile(h, b)].astype(F32)
            normed = m * inv
            out_ref[tile(h, b)] = (normed * gain).astype(BF16)
            gain_rows[h] = gain_rows[h] + jnp.sum((up * normed).reshape(rows_blk // 8, 8, D), axis=0)
            grad = gain * up * inv - m * factor
            gmix[c] = grad
            suffix_blk[h, b] = dot3(split(grad.T), split(solved[c]))
    put(ss, [sum(suffix_blk[h, b] for b in range(blocks)) for h in range(heads)] + gain_rows)
    scan_s.start(0)

    for c, (h, b) in enumerate(chains):
        key = k_ref[tile(h, b)]
        pair = split(gmix[c])
        score = split(jnp.where(lower, dot(side(pair), vt2[c]), 0.0))
        rhs = dot3(pair, split(assoc_all[h, b].T)) + dot(score[0], key) + dot(score[1], key)
        start_cg(c, rhs)
    solve(scan_s)

    pair_blk = {}
    for c, (h, b) in enumerate(chains):
        adj = x_s[c]
        gq_ref[tile(h, b)] = adj.astype(BF16)
        one = dot3(split(adj.T), split(solved[c]))
        pair_blk[h, b] = one + one.T
    put(ps, pack_sym([sum(pair_blk[h, b] for b in range(blocks)) for h in range(heads)]))
    scan_p.start(0)

    gain_total = scan_s.total()
    for h in range(heads):
        rows = gain_total[heads * D + 8 * h:heads * D + 8 * h + 8, :]
        gg_ref[:, pl.ds(h * D, D)] = jnp.sum(rows, axis=0, keepdims=True)

    done = 0
    for h in range(heads):
        run = se[pl.ds(h * D, D), :]
        for b in reversed(range(blocks)):
            c = h * blocks + b
            key = k_ref[tile(h, b)]
            value = v_ref[tile(h, b)]
            sol, adj, grad = split(solved[c]), split(x_s[c]), split(gmix[c])
            key_sol = split(jnp.where(upper, dot_rows(k2[c], side(sol)), 0.0))
            cross = split(jnp.where(
                upper,
                dot_rows(side([value, value]), side(grad)) - dot_rows(k2[c], side(adj)),
                0.0,
            ))
            suf = split(run)
            suf_t = split(run.T)
            gv = dot(key, suf_t[0]) + dot(key, suf_t[1]) + dot3(key_sol, grad)
            gv_ref[tile(h, b)] = gv.astype(BF16)
            gk_loc[c] = (
                dot(value, suf[0]) + dot(value, suf[1]) + dot3(cross, sol) - dot3(key_sol, adj)
            )
            run = run + suffix_blk[h, b]
            if done < rounds:
                scan_p.finish(done)
                done += 1
    while done < rounds:
        scan_p.finish(done)
        done += 1
    pairs = unpack_sym(pe, heads)
    for h in range(heads):
        run = pairs[h]
        for b in reversed(range(blocks)):
            c = h * blocks + b
            key = k_ref[tile(h, b)]
            high, low = split(run)
            gk_ref[tile(h, b)] = (gk_loc[c] - dot(key, high) - dot(key, low)).astype(BF16)
            run = run + pair_blk[h, b]


def per_device(n_seq, n_head, queries, keys, values, ridge, gain, grad_out):
    tok = queries.shape[0]
    heads = ridge.shape[0]
    rounds = n_seq.bit_length() - 1
    chains = heads * (tok // BLOCK_ROWS)
    rows = BLOCK_ROWS
    sym = sym_rows(heads)
    suf = heads * (D + 8)
    vm = pltpu.VMEM

    def state(count):
        return [vm((rounds, count, D), F32), vm((rounds, count, D), F32), vm((count, D), F32)]

    big = [vm((chains, rows, D), F32)] * 9
    wide = jax.ShapeDtypeStruct((tok, heads * D), BF16)
    spec = pl.BlockSpec(memory_space=pltpu.VMEM)
    outs = pl.pallas_call(
        functools.partial(kernel, n_seq, n_head, heads, tok),
        out_shape=[wide, wide, wide, wide, jax.ShapeDtypeStruct((1, heads * D), F32)],
        in_specs=[spec, spec, spec, pl.BlockSpec(memory_space=pltpu.SMEM), spec, spec],
        out_specs=[spec] * 5,
        scratch_shapes=[
            vm((chains, 2 * D, rows), BF16),
            vm((chains, 2 * D, rows), BF16),
            vm((chains, rows, 2 * D), BF16),
            vm((chains, 2 * D, D), BF16),
            vm((chains, D, D), BF16),
        ]
        + big
        + state(sym) + state(heads * D) + state(suf) + state(sym)
        + [
            vm((8, tok), F32),
            vm((n_head - 1, 8, tok), F32),
            pltpu.SemaphoreType.DMA((4, rounds)),
            pltpu.SemaphoreType.DMA((4, rounds)),
            pltpu.SemaphoreType.DMA((n_head - 1,)),
            pltpu.SemaphoreType.DMA((n_head - 1,)),
        ],
        compiler_params=pltpu.CompilerParams(
            collective_id=0, has_side_effects=True, vmem_limit_bytes=40 * 2**20
        ),
    )(queries, keys, values, ridge, gain.reshape(1, -1), grad_out)
    return (*outs[:4], outs[4].reshape(-1))


def solution(mesh):
    n_seq, n_head = mesh.shape["seq"], mesh.shape["head"]
    wide = P("seq", "head")
    return jax.shard_map(
        functools.partial(per_device, n_seq, n_head),
        mesh=mesh,
        in_specs=(wide, wide, wide, P("head"), P("head"), wide),
        out_specs=(wide, wide, wide, wide, P("head")),
        check_vma=False,
    )
```
